32 devices in a mesh: seq: 4 (over x, core), expert: 8 (over z, y).
Axes of the slice: x: 2, y: 2, z: 4, core: 2. Of those that a mesh axis runs over, the one named last changes fastest.
Arguments:
- queries: bfloat16 [8, 512, 2048], P('expert', 'seq'), may hold values from -8 to 8
- keys: bfloat16 [8, 512, 2048], P('expert', 'seq'), may hold values from -8 to 8
- values: bfloat16 [8, 512, 2048], P('expert', 'seq'), may hold values from -12 to 12
- hidden: bfloat16 [8, 512, 2048], P('expert', 'seq'), may hold values from -6 to 6
- out_proj: bfloat16 [2048, 2048], P('expert'), may hold values from -0.125 to 0.125
- ln_gain: float32 [2048], replicated, may hold values from 0.1 to 1.9
- w_router: bfloat16 [2048, 16], replicated, may hold values from -0.125 to 0.125
- routes: int32 [8, 512, 2], P('expert', 'seq'), may hold values from 0 to 15, all different within a row; in each aligned block of 128 rows (0 to 127, 128 to 255, ..., all dimensions but the last counted through in order) at most 32 rows name the same one
- w_in: bfloat16 [32, 2048, 2048], P(('seq', 'expert')), may hold values from -0.125 to 0.125
- w_out: bfloat16 [32, 2048, 2048], P(('seq', 'expert')), may hold values from -0.09375 to 0.09375
Outputs:
- layer_out: bfloat16 [8, 512, 2048], P('expert', 'seq')
The draws below stay inside these ranges and needn't reach their ends.
Inputs may be any that keep to these rules, and one draw needn't show every extreme that they name: `routes`: each token names two different experts. Among the 128 tokens of one device (rows in order of document, then position) no expert is named by more than 32 tokens, and in some such blocks one expert is named by exactly 32.
All inputs are finite; a program needn't handle non-finite values.
Results may differ from the reference program's by a relative error of at most 0.007.
Values may be sent and summed in bfloat16 or wider, within the bound.
No kernel may reach another device: no remote copies, remote signals or barrier semaphores. Data moves between devices by JAX's collectives and lax.ppermute only.
A program may use at most 128 MiB of HBM per device.

```python
import math
import jax
import jax.numpy as jnp
import numpy as np
from jax import lax

D = 2048
HEADS = 16
HEAD_DIM = 128
FF = 4096
TOK_DEV = 128
SRC_DEV = 128
EXPERTS = 16
DOCS = 8
TGT = 512
SRC = 512
CAP = 32
N_SEQ = 4
N_EXPERT = 8


def draw_queries(key, part):
    own_key = jax.random.fold_in(key, 11)
    drawn = jnp.clip(jax.random.normal(own_key, (DOCS, TGT, D), jnp.float32), -8.0, 8.0)
    return drawn.astype(jnp.bfloat16)


def draw_keys(key, part):
    own_key = jax.random.fold_in(key, 23)
    drawn = jnp.clip(2.0 * jax.random.normal(own_key, (DOCS, SRC, D), jnp.float32), -8.0, 8.0)
    return drawn.astype(jnp.bfloat16)


def steps_of(key, extent, shards, low, high):
    level = 1.0
    for axis_at, parts in shards:
        draws = jax.random.uniform(jax.random.fold_in(jax.random.fold_in(key, 6), axis_at), (parts,), jnp.float32, low / len(shards), high / len(shards))
        level = level * jnp.repeat(jnp.exp(draws), extent[axis_at] // parts).reshape((-1,) + (1,) * (len(extent) - 1 - axis_at))
    return level


def deal_out(stream_key, own, number, rows, number_of, top, limit, skew):
    ranking = jax.random.permutation(stream_key, number_of)
    heavy_load, ordinary = load_shares(number_of, rows * top, limit, skew, True), load_shares(number_of, rows * top, limit, skew, False)
    places = jnp.arange(number_of)

    def named(lengths, rotation):
        used = int((lengths > 0).sum())
        fixed = max(1, used // 4)
        passed = fixed + (places - fixed + rotation * (used - fixed)) % max(1, number_of - fixed)
        return jnp.zeros((number_of,), jnp.int32).at[ranking[jnp.where(places < fixed, places, passed)]].set(jnp.asarray(lengths, jnp.int32))

    lengths = jnp.where(number % 4 == 0, named(heavy_load, number // 4), named(ordinary, number - number // 4 - 1))
    mixed = jax.random.permutation(jax.random.fold_in(own, 3), number_of)
    source_of, sink = mixed[0:number_of // 2 * 2:2], mixed[1:number_of // 2 * 2:2]
    slack = jnp.minimum(lengths[source_of] - 1, limit - lengths[sink]) // 2
    slack = jnp.where((source_of == ranking[0]) | (sink == ranking[0]) | (lengths[sink] == 0), 0, jnp.maximum(slack, 0))
    passed = jax.random.randint(jax.random.fold_in(own, 4), (number_of // 2,), 0, 1 << 20) % (slack + 1)
    lengths = lengths.at[source_of].add(-passed).at[sink].add(passed)
    labels = jnp.searchsorted(jnp.cumsum(lengths), jnp.arange(rows * top), side="right").astype(jnp.int32)
    listing = labels.reshape(top, rows).T
    listing = listing[jax.random.permutation(jax.random.fold_in(own, 1), rows)]
    rotation = jax.random.randint(jax.random.fold_in(own, 2), (rows, 1), 0, top)
    return jnp.take_along_axis(listing, (jnp.arange(top)[None, :] + rotation) % top, axis=1)


def load_shares(count, total, bound, lean, full):
    loads = [(1 << 20) // math.isqrt(grade ** lean) + 1 for grade in range(1, count + 1)]
    largest = bound if full else min(bound, max(-(-total // count), total * loads[0] // sum(loads)))
    least = 1 if total - largest >= count - 1 else 0
    holding, spare = [largest] + [least] * (count - 1), total - largest - least * (count - 1)
    while spare > 0:
        free = [i for i in range(1, count) if holding[i] < largest] or [i for i in range(1, count) if holding[i] < bound]
        mass, remaining = sum([loads[i] for i in free]), spare
        for i in free:
            addition = min(bound - holding[i], max(1, remaining * loads[i] // mass), spare)
            holding[i] = holding[i] + addition
            spare = spare - addition
    return np.array(holding)


def gaussian(stream_key, extent, deviation, limit, cuts=(), kind=jnp.bfloat16):
    level = steps_of(stream_key, extent, cuts, -0.22, 0.18) if cuts else 1.0
    values = jax.random.normal(stream_key, extent, jnp.float32) * deviation * level
    return jnp.minimum(jnp.maximum(values, -limit), limit).astype(kind)


def setup_inputs(seed: int = 0) -> dict:
    streams_of = jax.random.split(jax.random.key(seed), 11)
    queries = draw_queries(jax.random.fold_in(streams_of[10], 71), 0)
    keys = draw_keys(jax.random.fold_in(streams_of[10], 71), 0)
    values = gaussian(streams_of[2], (DOCS, SRC, D), 3.0, 12.0, ((0, 8), (1, 4)))
    hidden = gaussian(streams_of[3], (DOCS, TGT, D), 1.0, 6.0, ((0, 8), (1, 4)))
    out_proj = gaussian(streams_of[4], (D, D), D ** -0.5, 0.125, ((0, 8),))
    ln_gain = jnp.clip(1.0 + 0.18 * jax.random.normal(streams_of[5], (D,), jnp.float32), 0.1, 1.9)
    w_router = gaussian(streams_of[6], (D, EXPERTS), D ** -0.5, 0.125)
    routes_keys = jax.random.split(jax.random.fold_in(streams_of[7], 1), DOCS * TGT // TOK_DEV)
    routes_turns = jax.random.permutation(jax.random.fold_in(streams_of[7], 3), DOCS * TGT // TOK_DEV)
    routes = jax.vmap(lambda own, number: deal_out(jax.random.fold_in(streams_of[7], 2), own, number, TOK_DEV, EXPERTS, 2, CAP, 2))(routes_keys, routes_turns).reshape((DOCS, TGT, 2))
    w_in = gaussian(streams_of[8], (2 * EXPERTS, D, FF // 2), D ** -0.5, 0.125, ((0, 32),))
    w_out = gaussian(streams_of[9], (2 * EXPERTS, FF // 2, D), FF ** -0.5, 0.09375, ((0, 32),))
    return {"queries": queries, "keys": keys, "values": values, "hidden": hidden, "out_proj": out_proj, "ln_gain": ln_gain, "w_router": w_router, "routes": routes, "w_in": w_in, "w_out": w_out}


NORM_EPS = 1e-05

def doc_attention(query_doc, key_doc, value_doc):
    query_heads = query_doc.reshape(TGT, HEADS, HEAD_DIM)
    key_heads = key_doc.reshape(N_SEQ, SRC_DEV, HEADS, HEAD_DIM)
    value_heads = value_doc.reshape(N_SEQ, SRC_DEV, HEADS, HEAD_DIM)
    scores = jnp.einsum('thd,bshd->hbts', query_heads, key_heads, precision=lax.Precision.HIGHEST) * HEAD_DIM ** (-0.5)
    peak_score = lax.optimization_barrier(jnp.max(scores, axis=3))
    weights = lax.optimization_barrier(jnp.exp(scores - peak_score[..., None]).astype(jnp.bfloat16)).astype(jnp.float32)
    block_total = lax.optimization_barrier(jnp.sum(weights, axis=3))
    block_value = jnp.einsum('hbts,bshd->hbtd', weights, value_heads, precision=lax.Precision.HIGHEST)
    top_peak = lax.optimization_barrier(jnp.max(peak_score, axis=1))
    new_scale = jnp.exp(peak_score - top_peak[:, None])
    numerator = lax.optimization_barrier(jnp.sum(new_scale[..., None] * block_value, axis=1))
    denominator = lax.optimization_barrier(jnp.sum(new_scale * block_total, axis=1))
    attended = (numerator / denominator[..., None]).transpose(1, 0, 2).reshape(TGT, D)
    return attended.astype(jnp.bfloat16)

def expert_table(normed_flat, ids_flat, w_in, w_out):
    pair_count = ids_flat.shape[0]
    one_hot = (ids_flat[:, None] == jnp.arange(EXPERTS, dtype=jnp.int32)[None, :]).astype(jnp.int32)
    rank = (lax.optimization_barrier(jnp.sum(jnp.cumsum(one_hot, axis=0) * one_hot, axis=1)) - 1).astype(jnp.int32)
    table_rows = N_SEQ * N_EXPERT * CAP
    token_of = (jnp.arange(pair_count, dtype=jnp.int32) // 2).astype(jnp.int32)
    table = jnp.full((EXPERTS, table_rows), normed_flat.shape[0], jnp.int32).at[ids_flat, rank].set(token_of)
    padded = jnp.concatenate([normed_flat, jnp.zeros((1, D), normed_flat.dtype)], axis=0)

    def one_expert(expert_index):
        gathered = padded[table[expert_index]].astype(jnp.float32)
        summed = jnp.zeros((table_rows, D), jnp.float32)
        for half_index in range(2):
            first_mat = w_in[2 * expert_index + half_index].astype(jnp.float32)
            inner_act = jnp.maximum(jnp.dot(gathered, first_mat, precision=lax.Precision.HIGHEST), 0.0)
            inner_act = lax.optimization_barrier(inner_act.astype(jnp.bfloat16)).astype(jnp.float32)
            second_mat = w_out[2 * expert_index + half_index].astype(jnp.float32)
            half_out = jnp.dot(inner_act, second_mat, precision=lax.Precision.HIGHEST)
            half_out = lax.optimization_barrier(half_out.astype(jnp.bfloat16)).astype(jnp.float32)
            summed = summed + half_out
        return summed
    outputs = lax.map(one_expert, jnp.arange(EXPERTS, dtype=jnp.int32))
    return outputs[ids_flat, rank]

def reference(queries, keys, values, hidden, out_proj, ln_gain, w_router, routes, w_in, w_out):

    def one_doc(doc_parts):
        query_doc, key_doc, value_doc = doc_parts
        return doc_attention(query_doc.astype(jnp.float32), key_doc.astype(jnp.float32), value_doc.astype(jnp.float32))
    attended = lax.map(one_doc, (queries, keys, values)).reshape(DOCS * TGT, D)
    residual = hidden.reshape(DOCS * TGT, D).astype(jnp.float32) + jnp.dot(attended, out_proj, preferred_element_type=jnp.float32)
    row_mean = lax.optimization_barrier(jnp.mean(residual, axis=1, keepdims=True))
    centered = residual - row_mean
    row_var = lax.optimization_barrier(jnp.mean(centered * centered, axis=1, keepdims=True))
    normed = (centered * lax.rsqrt(row_var + NORM_EPS) * ln_gain).astype(jnp.bfloat16)
    logits = jnp.dot(normed, w_router, preferred_element_type=jnp.float32)
    chosen = routes.reshape(DOCS * TGT, 2).astype(jnp.int32)
    picked = jnp.take_along_axis(logits, chosen, axis=1)
    gate_first = 1.0 / (1.0 + jnp.exp(picked[:, 1] - picked[:, 0]))
    gate_second = 1.0 / (1.0 + jnp.exp(picked[:, 0] - picked[:, 1]))
    expert_out = expert_table(normed, chosen.reshape(-1), w_in, w_out).reshape(DOCS * TGT, 2, D)
    layer_out = residual + gate_first[:, None] * expert_out[:, 0] + gate_second[:, None] * expert_out[:, 1]
    return layer_out.astype(jnp.bfloat16).reshape(DOCS, TGT, D)
```

```python
import functools

import jax
import jax.numpy as jnp
from jax import lax
from jax.experimental import pallas as pl
from jax.experimental.pallas import tpu as pltpu
from jax.sharding import PartitionSpec as P

HEADS = 16
HALVES = 2


NORM_EPS = 1e-05


def line_ring(count):
    return [0] + list(range(1, count, 2)) + [i for i in range(count - 1, 0, -1) if i % 2 == 0]


def swap_pairs(count, offset):
    return [(i, i ^ offset) for i in range(count)]


def after(block, earlier):
    return lax.optimization_barrier((block, *earlier))[0] if earlier else block


def attention_kernel(block_count, head_dim, *refs):
    query_ref, key_refs = refs[0], refs[1 : 1 + block_count]
    value_refs, out_ref = refs[1 + block_count : 1 + 2 * block_count], refs[-1]
    source_count = key_refs[0].shape[0]
    heads = [
        slice(at * head_dim, (at + 1) * head_dim) for at in range(query_ref.shape[1] // head_dim)
    ]
    ones = jnp.ones((source_count, head_dim), jnp.bfloat16)
    scores = [
        [
            lax.dot_general(
                query_ref[:, head],
                key_ref[:, head],
                (((1,), (1,)), ((), ())),
                preferred_element_type=jnp.float32,
            )
            for key_ref in key_refs
        ]
        for head in heads
    ]
    tops = [
        jnp.max(functools.reduce(jnp.maximum, blocks), axis=1, keepdims=True) for blocks in scores
    ]
    weights = [
        [jnp.exp((block - top) * head_dim ** (-0.5)).astype(jnp.bfloat16) for block in blocks]
        for blocks, top in zip(scores, tops)
    ]
    for head, blocks in zip(heads, weights):
        sums = sum(
            jnp.dot(
                block,
                jnp.concatenate([value_ref[:, head], ones], axis=1),
                preferred_element_type=jnp.float32,
            )
            for block, value_ref in zip(blocks, value_refs)
        )
        out_ref[:, head] = (sums[:, :head_dim] / sums[:, head_dim:]).astype(out_ref.dtype)


VMEM_BYTES = 56 * 1024 * 1024


def attention(query_rows, key_blocks, value_blocks, head_count, earlier):
    row_count, model_width = query_rows.shape
    head_dim = model_width // head_count
    width = model_width // 4
    operands = [query_rows, *key_blocks, *value_blocks]
    return pl.pallas_call(
        functools.partial(attention_kernel, len(key_blocks), head_dim),
        grid=(model_width // width,),
        in_specs=[pl.BlockSpec((block.shape[0], width), lambda i: (0, i)) for block in operands]
        + [pl.BlockSpec(memory_space=pl.ANY) for _ in earlier],
        out_specs=pl.BlockSpec((row_count, width), lambda i: (0, i)),
        out_shape=jax.ShapeDtypeStruct((row_count, model_width), jnp.bfloat16),
        compiler_params=pltpu.CompilerParams(vmem_limit_bytes=VMEM_BYTES),
        cost_estimate=pl.CostEstimate(flops=1000, bytes_accessed=1000, transcendentals=0),
    )(*operands, *earlier)


def expert_kernel(own_ref, other_ref, first_ref, second_ref, *refs):
    own_out, other_out, rows, inner, outs, first, second, weight_sems, row_sems, out_sems = refs[-10:]
    count = own_ref.shape[0]
    tile = first.shape[1] // 2

    def columns(at):
        return pl.ds(at * tile, tile)

    weight_copies = [
        pltpu.make_async_copy(
            source.at[:, columns(at)], held.at[:, columns(at)], weight_sems.at[2 * which + at]
        )
        for which, (source, held) in enumerate(((first_ref, first), (second_ref, second)))
        for at in range(2)
    ]
    row_copies = [
        pltpu.make_async_copy(own_ref, rows.at[:count], row_sems.at[0]),
        pltpu.make_async_copy(other_ref, rows.at[count:], row_sems.at[1]),
    ]
    out_copies = [
        pltpu.make_async_copy(
            outs.at[which * count : (which + 1) * count, columns(at)],
            target.at[:, columns(at)],
            out_sems.at[2 * at + which],
        )
        for at in range(2)
        for which, target in enumerate((own_out, other_out))
    ]
    for copy in row_copies + weight_copies[:2]:
        copy.start()
    for copy in row_copies:
        copy.wait()
    for at in range(2):
        weight_copies[2 + at].start()
        weight_copies[at].wait()
        act = jnp.dot(rows[...], first[:, columns(at)], preferred_element_type=jnp.float32)
        inner[:, columns(at)] = jnp.maximum(act, 0.0).astype(inner.dtype)
    for at in range(2):
        weight_copies[2 + at].wait()
        outs[:, columns(at)] = jnp.dot(
            inner[...], second[:, columns(at)], preferred_element_type=jnp.float32
        ).astype(outs.dtype)
        for copy in out_copies[2 * at : 2 * at + 2]:
            copy.start()
    for copy in out_copies:
        copy.wait()


def expert_half(own_rows, other_rows, first, second, earlier):
    count, model_width = own_rows.shape
    hidden_width = first.shape[1]
    out_type = jax.ShapeDtypeStruct((count, model_width), jnp.bfloat16)
    anywhere = pl.BlockSpec(memory_space=pl.ANY)
    return pl.pallas_call(
        expert_kernel,
        in_specs=[anywhere] * (4 + len(earlier)),
        out_specs=[anywhere, anywhere],
        out_shape=[out_type, out_type],
        scratch_shapes=[
            pltpu.VMEM((2 * count, model_width), jnp.bfloat16),
            pltpu.VMEM((2 * count, hidden_width), jnp.bfloat16),
            pltpu.VMEM((2 * count, model_width), jnp.bfloat16),
            pltpu.VMEM(first.shape, jnp.bfloat16),
            pltpu.VMEM(second.shape, jnp.bfloat16),
            pltpu.SemaphoreType.DMA((4,)),
            pltpu.SemaphoreType.DMA((2,)),
            pltpu.SemaphoreType.DMA((4,)),
        ],
        compiler_params=pltpu.CompilerParams(vmem_limit_bytes=VMEM_BYTES),
        cost_estimate=pl.CostEstimate(flops=1000, bytes_accessed=1000, transcendentals=0),
    )(own_rows, other_rows, first, second, *earlier)


def on_device(
    seq_count, expert_dev, queries, keys, values, hidden, out_proj, ln_gain, w_router, routes, w_in, w_out
):
    row_count, model_width = queries.shape[1:]
    expert_count = w_router.shape[1]
    slot_count = 4 * row_count // expert_count
    planes = expert_dev // HALVES
    seq_at = lax.axis_index("seq")
    expert_at = lax.axis_index("expert")
    plane, half = expert_at // HALVES, expert_at % HALVES
    core = seq_at % 2

    ring = line_ring(planes)
    ring_pairs = [
        [
            (ring[i] * HALVES + j, ring[(i + hop) % planes] * HALVES + j)
            for i in range(planes)
            for j in range(HALVES)
        ]
        for hop in range(planes)
    ]
    place_of = {ring[i]: i for i in range(planes)}
    source_plane = [
        sum(
            jnp.where(plane == i, ring[(place_of[i] - step) % planes], 0) for i in range(planes)
        )
        for step in range(planes)
    ]
    half_pairs = swap_pairs(expert_dev, 1)
    core_pairs = swap_pairs(seq_count, 1)

    def around(block, hop=1):
        with jax.named_scope("ring"):
            return lax.ppermute(block, "expert", ring_pairs[hop])

    def other_half(block):
        with jax.named_scope("half"):
            return lax.ppermute(block, "expert", half_pairs)

    def other_core(block):
        with jax.named_scope("core"):
            return lax.ppermute(block, "seq", core_pairs)

    chosen = routes[0].reshape(-1)
    expert_ids = jnp.arange(expert_count, dtype=jnp.int32)
    one_hot = (chosen[:, None] == expert_ids[None, :]).astype(jnp.int32)
    slot_index = jnp.sum(jnp.cumsum(one_hot, axis=0) * one_hot, axis=1) - 1
    target = (chosen * slot_count + slot_index).reshape(row_count, 2)

    depth = out_proj.shape[0]
    half_width = model_width // 2
    proj_part = lax.dynamic_slice_in_dim(out_proj, core * half_width, half_width, axis=1)
    proj_blocks, proj_others = [proj_part], []
    sources = [keys[0], values[0], target.T]
    gathered = [[source] + [None] * (seq_count - 1) for source in sources[:2]]
    hops = [(which, across) for which in range(2) for across in range(2, seq_count, 2)]
    for step in range(max(planes - 1, len(hops))):
        with jax.named_scope(f"gather_{step}"):
            arrived = []
            if step < planes - 1:
                arrived = [other_half(proj_blocks[step]), around(proj_blocks[step])]
            if step < len(hops):
                which, across = hops[step]
                arrived.append(
                    lax.ppermute(sources[which], "seq", swap_pairs(seq_count, across))
                )
            *sources, = lax.optimization_barrier((*sources, *arrived))
            sources, arrived = sources[:3], sources[3:]
            if step < planes - 1:
                proj_others.append(arrived[0])
                proj_blocks.append(arrived[1])
            if step < len(hops):
                gathered[which][across] = arrived[-1]
            if step == 0:
                targets = [target.T] + [around(sources[2], hop) for hop in range(1, planes)]
    depth_cut = depth // 2 if planes > 1 else depth
    last_other = [other_half(proj_blocks[-1][:depth_cut])]
    if planes > 1:
        last_other.append(around(proj_others[-1][depth_cut:]))
    for blocks in gathered:
        for across in range(0, seq_count, 2):
            blocks[across + 1] = other_core(blocks[across])
    key_blocks, value_blocks = gathered
    attended = attention(
        queries[0], key_blocks, value_blocks, HEADS, []
    )
    both_attended = jnp.concatenate([attended, other_core(attended)], axis=0)
    projected = 0.0
    for step in range(planes):
        own_at = source_plane[step] * HALVES + half
        other_at = source_plane[step] * HALVES + (1 - half)
        pieces = [(own_at * depth, proj_blocks[step])]
        if step < planes - 1:
            pieces.append((other_at * depth, proj_others[step]))
        else:
            pieces += [
                (other_at * depth + cut, block)
                for cut, block in zip((0, depth_cut), last_other)
            ]
        for at, block in pieces:
            columns = lax.dynamic_slice_in_dim(both_attended, at, block.shape[0], axis=1)
            projected = projected + jnp.dot(columns, block, preferred_element_type=jnp.float32)
    mine, theirs = projected[:row_count], other_core(projected[row_count:])
    projected = jnp.concatenate(
        [jnp.where(core == 0, mine, theirs), jnp.where(core == 0, theirs, mine)], axis=1
    )

    residual = hidden[0].astype(jnp.float32) + projected
    row_mean = jnp.mean(residual, axis=1, keepdims=True)
    centered = residual - row_mean
    row_var = jnp.mean(centered * centered, axis=1, keepdims=True)
    normed = (centered * lax.rsqrt(row_var + NORM_EPS) * ln_gain).astype(jnp.bfloat16)

    block_rows = seq_count * slot_count
    pair_rows = 2 * slot_count
    slot_ids = jnp.arange(block_rows, dtype=jnp.int32)
    served = jnp.bitwise_xor(slot_ids // slot_count, seq_at) * planes + plane
    served_target = served * slot_count + slot_ids % slot_count

    def exchange(rows):
        parts = [rows[i * slot_count : (i + 1) * slot_count] for i in range(seq_count)]
        for i in range(1, seq_count):
            parts[i] = lax.ppermute(parts[i], "seq", swap_pairs(seq_count, i))
        return jnp.concatenate(parts, axis=0)

    with jax.named_scope("tokens"):
        blocks = [normed]
        for _ in range(1, planes):
            blocks.append(around(blocks[-1]))

    def around_add(passing, part):
        with jax.named_scope("back_home"):
            if passing is not None:
                part = part + around(passing).astype(jnp.float32)
            return part.astype(jnp.bfloat16)

    matches, slot_rows, other_rows = [], [], []
    for step in range(planes):
        with jax.named_scope(f"out_{step}"):
            target = targets[step].T
            matches.append([target[:, k : k + 1] == served_target[None, :] for k in range(2)])
            place_map = (matches[step][0] | matches[step][1]).astype(jnp.bfloat16)
            slots = jnp.einsum(
                "ts,td->sd", place_map, blocks[step], preferred_element_type=jnp.float32
            ).astype(jnp.bfloat16)
            slot_rows.append(exchange(slots))
            other_rows.append(other_half(slot_rows[step]))

    def expert_step(step, earlier):
        with jax.named_scope(f"expert_{step}"):
            return expert_half(slot_rows[step], other_rows[step], w_in[0], w_out[0], earlier)

    def combine(step, outs, later):
        with jax.named_scope(f"back_{step}"):
            own_out, other_out = outs
            own_out = after(own_out, later)
            out_sum = own_out.astype(jnp.float32) + other_half(other_out).astype(jnp.float32)
            returned = exchange(out_sum.astype(jnp.bfloat16))
            logits = jnp.dot(blocks[step], w_router, preferred_element_type=jnp.float32)
            named = (targets[step].T // slot_count)[:, :, None] == expert_ids[None, None, :]
            picked = jnp.sum(jnp.where(named, logits[:, None, :], 0.0), axis=2)
            gate_first = 1.0 / (1.0 + jnp.exp(picked[:, 1:2] - picked[:, 0:1]))
            gate_second = 1.0 / (1.0 + jnp.exp(picked[:, 0:1] - picked[:, 1:2]))
            gate_map = jnp.where(matches[step][0], gate_first, 0.0) + jnp.where(
                matches[step][1], gate_second, 0.0
            )
            gate_high = gate_map.astype(jnp.bfloat16)
            gate_low = (gate_map - gate_high.astype(jnp.float32)).astype(jnp.bfloat16)
            return jnp.dot(gate_high, returned, preferred_element_type=jnp.float32) + jnp.dot(
                gate_low, returned, preferred_element_type=jnp.float32
            )

    outs = [None] * planes
    passing, waiting = None, []
    for step in range(1, planes):
        ahead = slot_rows[step + 1 : step + 2]
        outs[step] = expert_step(step, ahead + other_rows[:1] if step == 1 else ahead)
        if step > 1:
            later = [outs[step][0], *other_rows[step + 1 : step + 2]]
            passing = around_add(passing, combine(step - 1, outs[step - 1], later))
            waiting = waiting or [passing]
    outs[0] = expert_step(0, waiting + [outs[-1][1]])
    if planes > 1:
        passing = around_add(passing, combine(planes - 1, outs[-1], outs[0][:1]))
    layer_out = residual + combine(0, outs[0], [])
    if planes > 1:
        layer_out = layer_out + around(passing).astype(jnp.float32)
    return layer_out.astype(jnp.bfloat16)[None]


def solution(mesh):
    seq_count, expert_dev = mesh.shape["seq"], mesh.shape["expert"]
    in_specs = (
        P("expert", "seq", None),
        P("expert", "seq", None),
        P("expert", "seq", None),
        P("expert", "seq", None),
        P("expert", None),
        P(),
        P(),
        P("expert", "seq", None),
        P(("seq", "expert"), None, None),
        P(("seq", "expert"), None, None),
    )
    out_specs = P("expert", "seq", None)

    def device_part(*arrays):
        return on_device(seq_count, expert_dev, *arrays)

    return jax.shard_map(
        device_part, mesh=mesh, in_specs=in_specs, out_specs=out_specs, check_vma=False
    )
```

```python
import functools

import jax
import jax.numpy as jnp
from jax import lax
from jax.experimental import pallas as pl
from jax.experimental.pallas import tpu as pltpu
from jax.sharding import PartitionSpec as P

HEADS = 16
HALVES = 2
TIES = {"E1": ["D0", "W2"], "E2": ["W3"], "H1": ["E2"], "H2": ["E3"], "H3": ["E0"], "E0": ["D1", "E3", "P1"], "X3": ["E0", "P2"], "S1": ["W0"], "Z2": ["W0"], "Z3": ["D0"]}
ECOST = 4000000000
ACOST = 1000


NORM_EPS = 1e-05


def line_ring(count):
    return [0] + list(range(1, count, 2)) + [i for i in range(count - 1, 0, -1) if i % 2 == 0]


def swap_pairs(count, offset):
    return [(i, i ^ offset) for i in range(count)]


def after(block, earlier):
    return lax.optimization_barrier((block, *earlier))[0] if earlier else block


def attention_kernel(block_count, head_dim, *refs):
    query_ref, key_refs = refs[0], refs[1 : 1 + block_count]
    value_refs, out_ref = refs[1 + block_count : 1 + 2 * block_count], refs[-1]
    source_count = key_refs[0].shape[0]
    heads = [
        slice(at * head_dim, (at + 1) * head_dim) for at in range(query_ref.shape[1] // head_dim)
    ]
    ones = jnp.ones((source_count, head_dim), jnp.bfloat16)
    scores = [
        [
            lax.dot_general(
                query_ref[:, head],
                key_ref[:, head],
                (((1,), (1,)), ((), ())),
                preferred_element_type=jnp.float32,
            )
            for key_ref in key_refs
        ]
        for head in heads
    ]
    tops = [
        jnp.max(functools.reduce(jnp.maximum, blocks), axis=1, keepdims=True) for blocks in scores
    ]
    weights = [
        [jnp.exp((block - top) * head_dim ** (-0.5)).astype(jnp.bfloat16) for block in blocks]
        for blocks, top in zip(scores, tops)
    ]
    for head, blocks in zip(heads, weights):
        sums = sum(
            jnp.dot(
                block,
                jnp.concatenate([value_ref[:, head], ones], axis=1),
                preferred_element_type=jnp.float32,
            )
            for block, value_ref in zip(blocks, value_refs)
        )
        out_ref[:, head] = (sums[:, :head_dim] / sums[:, head_dim:]).astype(out_ref.dtype)


VMEM_BYTES = 56 * 1024 * 1024


def attention(query_rows, key_blocks, value_blocks, head_count, earlier):
    row_count, model_width = query_rows.shape
    head_dim = model_width // head_count
    width = model_width // 4
    operands = [query_rows, *key_blocks, *value_blocks]
    return pl.pallas_call(
        functools.partial(attention_kernel, len(key_blocks), head_dim),
        grid=(model_width // width,),
        in_specs=[pl.BlockSpec((block.shape[0], width), lambda i: (0, i)) for block in operands]
        + [pl.BlockSpec(memory_space=pl.ANY) for _ in earlier],
        out_specs=pl.BlockSpec((row_count, width), lambda i: (0, i)),
        out_shape=jax.ShapeDtypeStruct((row_count, model_width), jnp.bfloat16),
        compiler_params=pltpu.CompilerParams(vmem_limit_bytes=VMEM_BYTES),
        cost_estimate=pl.CostEstimate(flops=ACOST, bytes_accessed=1000, transcendentals=0),
    )(*operands, *earlier)


def expert_kernel(own_ref, other_ref, first_ref, second_ref, *refs):
    own_out, other_out, rows, inner, outs, first, second, weight_sems, row_sems, out_sems = refs[-10:]
    count = own_ref.shape[0]
    tile = first.shape[1] // 2

    def columns(at):
        return pl.ds(at * tile, tile)

    weight_copies = [
        pltpu.make_async_copy(
            source.at[:, columns(at)], held.at[:, columns(at)], weight_sems.at[2 * which + at]
        )
        for which, (source, held) in enumerate(((first_ref, first), (second_ref, second)))
        for at in range(2)
    ]
    row_copies = [
        pltpu.make_async_copy(own_ref, rows.at[:count], row_sems.at[0]),
        pltpu.make_async_copy(other_ref, rows.at[count:], row_sems.at[1]),
    ]
    out_copies = [
        pltpu.make_async_copy(
            outs.at[which * count : (which + 1) * count, columns(at)],
            target.at[:, columns(at)],
            out_sems.at[2 * at + which],
        )
        for at in range(2)
        for which, target in enumerate((own_out, other_out))
    ]
    for copy in row_copies + weight_copies[:2]:
        copy.start()
    for copy in row_copies:
        copy.wait()
    for at in range(2):
        weight_copies[2 + at].start()
        weight_copies[at].wait()
        act = jnp.dot(rows[...], first[:, columns(at)], preferred_element_type=jnp.float32)
        inner[:, columns(at)] = jnp.maximum(act, 0.0).astype(inner.dtype)
    for at in range(2):
        weight_copies[2 + at].wait()
        outs[:, columns(at)] = jnp.dot(
            inner[...], second[:, columns(at)], preferred_element_type=jnp.float32
        ).astype(outs.dtype)
        for copy in out_copies[2 * at : 2 * at + 2]:
            copy.start()
    for copy in out_copies:
        copy.wait()


def expert_half(own_rows, other_rows, first, second, earlier):
    count, model_width = own_rows.shape
    hidden_width = first.shape[1]
    out_type = jax.ShapeDtypeStruct((count, model_width), jnp.bfloat16)
    anywhere = pl.BlockSpec(memory_space=pl.ANY)
    return pl.pallas_call(
        expert_kernel,
        in_specs=[anywhere] * (4 + len(earlier)),
        out_specs=[anywhere, anywhere],
        out_shape=[out_type, out_type],
        scratch_shapes=[
            pltpu.VMEM((2 * count, model_width), jnp.bfloat16),
            pltpu.VMEM((2 * count, hidden_width), jnp.bfloat16),
            pltpu.VMEM((2 * count, model_width), jnp.bfloat16),
            pltpu.VMEM(first.shape, jnp.bfloat16),
            pltpu.VMEM(second.shape, jnp.bfloat16),
            pltpu.SemaphoreType.DMA((4,)),
            pltpu.SemaphoreType.DMA((2,)),
            pltpu.SemaphoreType.DMA((4,)),
        ],
        compiler_params=pltpu.CompilerParams(vmem_limit_bytes=VMEM_BYTES),
        cost_estimate=pl.CostEstimate(flops=ECOST, bytes_accessed=1000, transcendentals=0),
    )(own_rows, other_rows, first, second, *earlier)


def on_device(
    seq_count, expert_dev, queries, keys, values, hidden, out_proj, ln_gain, w_router, routes, w_in, w_out
):
    row_count, model_width = queries.shape[1:]
    expert_count = w_router.shape[1]
    slot_count = 4 * row_count // expert_count
    planes = expert_dev // HALVES
    seq_at = lax.axis_index("seq")
    expert_at = lax.axis_index("expert")
    plane, half = expert_at // HALVES, expert_at % HALVES
    core = seq_at % 2

    ring = line_ring(planes)
    ring_pairs = [
        [
            (ring[i] * HALVES + j, ring[(i + hop) % planes] * HALVES + j)
            for i in range(planes)
            for j in range(HALVES)
        ]
        for hop in range(planes)
    ]
    place_of = {ring[i]: i for i in range(planes)}
    source_plane = [
        sum(
            jnp.where(plane == i, ring[(place_of[i] - step) % planes], 0) for i in range(planes)
        )
        for step in range(planes)
    ]
    half_pairs = swap_pairs(expert_dev, 1)
    core_pairs = swap_pairs(seq_count, 1)

    def around(block, hop=1):
        with jax.named_scope("ring"):
            return lax.ppermute(block, "expert", ring_pairs[hop])

    def other_half(block):
        with jax.named_scope("half"):
            return lax.ppermute(block, "expert", half_pairs)

    def other_core(block):
        with jax.named_scope("core"):
            return lax.ppermute(block, "seq", core_pairs)

    chosen = routes[0].reshape(-1)
    expert_ids = jnp.arange(expert_count, dtype=jnp.int32)
    one_hot = (chosen[:, None] == expert_ids[None, :]).astype(jnp.int32)
    slot_index = jnp.sum(jnp.cumsum(one_hot, axis=0) * one_hot, axis=1) - 1
    target = (chosen * slot_count + slot_index).reshape(row_count, 2)

    depth = out_proj.shape[0]
    half_width = model_width // 2
    proj_part = lax.dynamic_slice_in_dim(out_proj, core * half_width, half_width, axis=1)
    proj_blocks, proj_others = [proj_part], []
    sources = [keys[0], values[0], target.T]
    gathered = [[source] + [None] * (seq_count - 1) for source in sources[:2]]
    hops = [(which, across) for which in range(2) for across in range(2, seq_count, 2)]
    for step in range(max(planes - 1, len(hops))):
        with jax.named_scope(f"gather_{step}"):
            arrived = []
            if step < planes - 1:
                arrived = [other_half(proj_blocks[step]), around(proj_blocks[step])]
            if step < len(hops):
                which, across = hops[step]
                arrived.append(
                    lax.ppermute(sources[which], "seq", swap_pairs(seq_count, across))
                )
            *sources, = lax.optimization_barrier((*sources, *arrived))
            sources, arrived = sources[:3], sources[3:]
            if step < planes - 1:
                proj_others.append(arrived[0])
                proj_blocks.append(arrived[1])
            if step < len(hops):
                gathered[which][across] = arrived[-1]
            if step == 0:
                targets = [target.T] + [around(sources[2], hop) for hop in range(1, planes)]
    depth_cut = depth // 2 if planes > 1 else depth
    last_other = [other_half(proj_blocks[-1][:depth_cut])]
    if planes > 1:
        last_other.append(around(proj_others[-1][depth_cut:]))
    for blocks in gathered:
        for across in range(0, seq_count, 2):
            blocks[across + 1] = other_core(blocks[across])
    key_blocks, value_blocks = gathered
    attended = attention(
        queries[0], key_blocks, value_blocks, HEADS, []
    )
    both_attended = jnp.concatenate([attended, other_core(attended)], axis=0)
    projected = 0.0
    for step in range(planes):
        own_at = source_plane[step] * HALVES + half
        other_at = source_plane[step] * HALVES + (1 - half)
        pieces = [(own_at * depth, proj_blocks[step])]
        if step < planes - 1:
            pieces.append((other_at * depth, proj_others[step]))
        else:
            pieces += [
                (other_at * depth + cut, block)
                for cut, block in zip((0, depth_cut), last_other)
            ]
        for at, block in pieces:
            columns = lax.dynamic_slice_in_dim(both_attended, at, block.shape[0], axis=1)
            projected = projected + jnp.dot(columns, block, preferred_element_type=jnp.float32)
    mine, theirs = projected[:row_count], other_core(projected[row_count:])
    projected = jnp.concatenate(
        [jnp.where(core == 0, mine, theirs), jnp.where(core == 0, theirs, mine)], axis=1
    )

    residual = hidden[0].astype(jnp.float32) + projected
    row_mean = jnp.mean(residual, axis=1, keepdims=True)
    centered = residual - row_mean
    row_var = jnp.mean(centered * centered, axis=1, keepdims=True)
    normed = (centered * lax.rsqrt(row_var + NORM_EPS) * ln_gain).astype(jnp.bfloat16)

    block_rows = seq_count * slot_count
    pair_rows = 2 * slot_count
    slot_ids = jnp.arange(block_rows, dtype=jnp.int32)
    served = jnp.bitwise_xor(slot_ids // slot_count, seq_at) * planes + plane
    served_target = served * slot_count + slot_ids % slot_count

    def exchange(rows):
        parts = [rows[i * slot_count : (i + 1) * slot_count] for i in range(seq_count)]
        for i in range(1, seq_count):
            parts[i] = lax.ppermute(parts[i], "seq", swap_pairs(seq_count, i))
        return jnp.concatenate(parts, axis=0)

    made = {}

    def get(name):
        if name not in made:
            made[name] = MAKE[name[0]](int(name[1:]), [get(other) for other in TIES.get(name, []) if int(other[1:]) < planes])
        return made[name]

    def tied(value, others):
        return after(value, [other[0] if isinstance(other, tuple) else other for other in others])

    def token_block(step, ties):
        return around(tied(get(f"Z{step - 1}"), ties)) if step else normed

    def matches(step):
        target = targets[step].T
        return [target[:, k : k + 1] == served_target[None, :] for k in range(2)]

    def slot_block(step, ties):
        match = matches(step)
        return jnp.einsum(
            "ts,td->sd",
            (match[0] | match[1]).astype(jnp.bfloat16),
            tied(get(f"Z{step}"), ties),
            preferred_element_type=jnp.float32,
        ).astype(jnp.bfloat16)

    def expert_rows(step, ties):
        return exchange(tied(get(f"S{step}"), ties))

    def other_rows(step, ties):
        return other_half(tied(get(f"W{step}"), ties))

    def expert_out(step, ties):
        own, other = get(f"W{step}"), get(f"D{step}")
        ties = [tie[0] if isinstance(tie, tuple) else tie for tie in ties]
        return tuple(expert_half(own, other, w_in[0], w_out[0], ties))

    def other_out(step, ties):
        return other_half(tied(get(f"E{step}")[1], ties))

    def both_halves(step, ties):
        own = tied(get(f"E{step}")[0], ties)
        both = own.astype(jnp.float32) + get(f"R{step}").astype(jnp.float32)
        return both.astype(jnp.bfloat16)

    def returned_rows(step, ties):
        return exchange(tied(get(f"H{step}"), ties))

    def gated_part(step, ties):
        returned = tied(get(f"X{step}"), ties)
        match = matches(step)
        logits = jnp.dot(get(f"Z{step}"), w_router, preferred_element_type=jnp.float32)
        named = (targets[step].T // slot_count)[:, :, None] == expert_ids[None, None, :]
        picked = jnp.sum(jnp.where(named, logits[:, None, :], 0.0), axis=2)
        gate_first = 1.0 / (1.0 + jnp.exp(picked[:, 1:2] - picked[:, 0:1]))
        gate_second = 1.0 / (1.0 + jnp.exp(picked[:, 0:1] - picked[:, 1:2]))
        gate_map = jnp.where(match[0], gate_first, 0.0) + jnp.where(match[1], gate_second, 0.0)
        gate_high = gate_map.astype(jnp.bfloat16)
        gate_low = (gate_map - gate_high.astype(jnp.float32)).astype(jnp.bfloat16)
        return jnp.dot(gate_high, returned, preferred_element_type=jnp.float32) + jnp.dot(
            gate_low, returned, preferred_element_type=jnp.float32
        )

    def passed_sum(step, ties):
        part = get(f"G{step}")
        if step > 1:
            part = part + around(get(f"P{step - 1}")).astype(jnp.float32)
        return tied(part.astype(jnp.bfloat16), ties)

    MAKE = {
        "Z": token_block,
        "S": slot_block,
        "W": expert_rows,
        "D": other_rows,
        "E": expert_out,
        "R": other_out,
        "H": both_halves,
        "X": returned_rows,
        "G": gated_part,
        "P": passed_sum,
    }
    layer_out = residual + get("G0")
    if planes > 1:
        last = get(f"P{planes - 1}")
        with jax.named_scope("home"):
            layer_out = layer_out + around(last).astype(jnp.float32)
    return layer_out.astype(jnp.bfloat16)[None]


def solution(mesh):
    seq_count, expert_dev = mesh.shape["seq"], mesh.shape["expert"]
    in_specs = (
        P("expert", "seq", None),
        P("expert", "seq", None),
        P("expert", "seq", None),
        P("expert", "seq", None),
        P("expert", None),
        P(),
        P(),
        P("expert", "seq", None),
        P(("seq", "expert"), None, None),
        P(("seq", "expert"), None, None),
    )
    out_specs = P("expert", "seq", None)

    def device_part(*arrays):
        return on_device(seq_count, expert_dev, *arrays)

    return jax.shard_map(
        device_part, mesh=mesh, in_specs=in_specs, out_specs=out_specs, check_vma=False
    )
```

```python
import functools

import jax
import jax.numpy as jnp
from jax import lax
from jax.experimental import pallas as pl
from jax.experimental.pallas import tpu as pltpu
from jax.sharding import PartitionSpec as P

HEADS = 16
HALVES = 2
TIES = {"E1": ["D0", "W2"], "E2": ["W3"], "H1": ["E2"], "H2": ["P1"], "H3": ["E0"], "E0": ["D1", "E3", "P1"], "X3": ["E0", "P2"], "S1": ["W0"], "Z2": ["W0"], "Z3": ["D0"], "G1": ["E3"], "E3": ["H1"]}
ECOST = 4000000000
ACOST = 1000


NORM_EPS = 1e-05


def line_ring(count):
    return [0] + list(range(1, count, 2)) + [i for i in range(count - 1, 0, -1) if i % 2 == 0]


def swap_pairs(count, offset):
    return [(i, i ^ offset) for i in range(count)]


def after(block, earlier):
    return lax.optimization_barrier((block, *earlier))[0] if earlier else block


def attention_kernel(block_count, head_dim, *refs):
    query_ref, key_refs = refs[0], refs[1 : 1 + block_count]
    value_refs, out_ref = refs[1 + block_count : 1 + 2 * block_count], refs[-1]
    source_count = key_refs[0].shape[0]
    heads = [
        slice(at * head_dim, (at + 1) * head_dim) for at in range(query_ref.shape[1] // head_dim)
    ]
    ones = jnp.ones((source_count, head_dim), jnp.bfloat16)
    scores = [
        [
            lax.dot_general(
                query_ref[:, head],
                key_ref[:, head],
                (((1,), (1,)), ((), ())),
                preferred_element_type=jnp.float32,
            )
            for key_ref in key_refs
        ]
        for head in heads
    ]
    tops = [
        jnp.max(functools.reduce(jnp.maximum, blocks), axis=1, keepdims=True) for blocks in scores
    ]
    weights = [
        [jnp.exp((block - top) * head_dim ** (-0.5)).astype(jnp.bfloat16) for block in blocks]
        for blocks, top in zip(scores, tops)
    ]
    for head, blocks in zip(heads, weights):
        sums = sum(
            jnp.dot(
                block,
                jnp.concatenate([value_ref[:, head], ones], axis=1),
                preferred_element_type=jnp.float32,
            )
            for block, value_ref in zip(blocks, value_refs)
        )
        out_ref[:, head] = (sums[:, :head_dim] / sums[:, head_dim:]).astype(out_ref.dtype)


VMEM_BYTES = 56 * 1024 * 1024
EXPERT_BYTES = 48 * 1024 * 1024


def attention(query_rows, key_blocks, value_blocks, head_count, earlier):
    row_count, model_width = query_rows.shape
    head_dim = model_width // head_count
    width = model_width // 4
    operands = [query_rows, *key_blocks, *value_blocks]
    return pl.pallas_call(
        functools.partial(attention_kernel, len(key_blocks), head_dim),
        grid=(model_width // width,),
        in_specs=[pl.BlockSpec((block.shape[0], width), lambda i: (0, i)) for block in operands]
        + [pl.BlockSpec(memory_space=pl.ANY) for _ in earlier],
        out_specs=pl.BlockSpec((row_count, width), lambda i: (0, i)),
        out_shape=jax.ShapeDtypeStruct((row_count, model_width), jnp.bfloat16),
        compiler_params=pltpu.CompilerParams(vmem_limit_bytes=VMEM_BYTES),
        cost_estimate=pl.CostEstimate(flops=ACOST, bytes_accessed=1000, transcendentals=0),
    )(*operands, *earlier)


def expert_kernel(own_ref, other_ref, first_ref, second_ref, *refs):
    own_out, other_out, rows, inner, outs, first, second, weight_sems, row_sems, out_sems = refs[-10:]
    count = own_ref.shape[0]
    tile = first.shape[1] // 2

    def columns(at):
        return pl.ds(at * tile, tile)

    weight_copies = [
        pltpu.make_async_copy(
            source.at[:, columns(at)], held.at[:, columns(at)], weight_sems.at[2 * which + at]
        )
        for which, (source, held) in enumerate(((first_ref, first), (second_ref, second)))
        for at in range(2)
    ]
    row_copies = [
        pltpu.make_async_copy(own_ref, rows.at[:count], row_sems.at[0]),
        pltpu.make_async_copy(other_ref, rows.at[count:], row_sems.at[1]),
    ]
    out_copies = [
        pltpu.make_async_copy(
            outs.at[which * count : (which + 1) * count, columns(at)],
            target.at[:, columns(at)],
            out_sems.at[2 * at + which],
        )
        for at in range(2)
        for which, target in enumerate((own_out, other_out))
    ]
    for copy in row_copies + weight_copies[:2]:
        copy.start()
    for copy in row_copies:
        copy.wait()
    for at in range(2):
        weight_copies[2 + at].start()
        weight_copies[at].wait()
        act = jnp.dot(rows[...], first[:, columns(at)], preferred_element_type=jnp.float32)
        inner[:, columns(at)] = jnp.maximum(act, 0.0).astype(inner.dtype)
    for at in range(2):
        weight_copies[2 + at].wait()
        outs[:, columns(at)] = jnp.dot(
            inner[...], second[:, columns(at)], preferred_element_type=jnp.float32
        ).astype(outs.dtype)
        for copy in out_copies[2 * at : 2 * at + 2]:
            copy.start()
    for copy in out_copies:
        copy.wait()


def expert_half(own_rows, other_rows, first, second, earlier):
    count, model_width = own_rows.shape
    hidden_width = first.shape[1]
    out_type = jax.ShapeDtypeStruct((count, model_width), jnp.bfloat16)
    anywhere = pl.BlockSpec(memory_space=pl.ANY)
    return pl.pallas_call(
        expert_kernel,
        in_specs=[anywhere] * (4 + len(earlier)),
        out_specs=[anywhere, anywhere],
        out_shape=[out_type, out_type],
        scratch_shapes=[
            pltpu.VMEM((2 * count, model_width), jnp.bfloat16),
            pltpu.VMEM((2 * count, hidden_width), jnp.bfloat16),
            pltpu.VMEM((2 * count, model_width), jnp.bfloat16),
            pltpu.VMEM(first.shape, jnp.bfloat16),
            pltpu.VMEM(second.shape, jnp.bfloat16),
            pltpu.SemaphoreType.DMA((4,)),
            pltpu.SemaphoreType.DMA((2,)),
            pltpu.SemaphoreType.DMA((4,)),
        ],
        compiler_params=pltpu.CompilerParams(vmem_limit_bytes=EXPERT_BYTES),
        cost_estimate=pl.CostEstimate(flops=ECOST, bytes_accessed=1000, transcendentals=0),
    )(own_rows, other_rows, first, second, *earlier)


def on_device(
    seq_count, expert_dev, queries, keys, values, hidden, out_proj, ln_gain, w_router, routes, w_in, w_out
):
    row_count, model_width = queries.shape[1:]
    expert_count = w_router.shape[1]
    slot_count = 4 * row_count // expert_count
    planes = expert_dev // HALVES
    seq_at = lax.axis_index("seq")
    expert_at = lax.axis_index("expert")
    plane, half = expert_at // HALVES, expert_at % HALVES
    core = seq_at % 2

    ring = line_ring(planes)
    ring_pairs = [
        [
            (ring[i] * HALVES + j, ring[(i + hop) % planes] * HALVES + j)
            for i in range(planes)
            for j in range(HALVES)
        ]
        for hop in range(planes)
    ]
    place_of = {ring[i]: i for i in range(planes)}
    source_plane = [
        sum(
            jnp.where(plane == i, ring[(place_of[i] - step) % planes], 0) for i in range(planes)
        )
        for step in range(planes)
    ]
    half_pairs = swap_pairs(expert_dev, 1)
    core_pairs = swap_pairs(seq_count, 1)

    def around(block, hop=1):
        with jax.named_scope("ring"):
            return lax.ppermute(block, "expert", ring_pairs[hop])

    def other_half(block):
        with jax.named_scope("half"):
            return lax.ppermute(block, "expert", half_pairs)

    def other_core(block):
        with jax.named_scope("core"):
            return lax.ppermute(block, "seq", core_pairs)

    chosen = routes[0].reshape(-1)
    expert_ids = jnp.arange(expert_count, dtype=jnp.int32)
    one_hot = (chosen[:, None] == expert_ids[None, :]).astype(jnp.int32)
    slot_index = jnp.sum(jnp.cumsum(one_hot, axis=0) * one_hot, axis=1) - 1
    target = (chosen * slot_count + slot_index).reshape(row_count, 2)

    depth = out_proj.shape[0]
    half_width = model_width // 2
    proj_part = lax.dynamic_slice_in_dim(out_proj, core * half_width, half_width, axis=1)
    proj_blocks, proj_others = [proj_part], []
    sources = [keys[0], values[0], target.T]
    gathered = [[source] + [None] * (seq_count - 1) for source in sources[:2]]
    hops = [(which, across) for which in range(2) for across in range(2, seq_count, 2)]
    for step in range(max(planes - 1, len(hops))):
        with jax.named_scope(f"gather_{step}"):
            arrived = []
            if step < planes - 1:
                arrived = [other_half(proj_blocks[step]), around(proj_blocks[step])]
            if step < len(hops):
                which, across = hops[step]
                arrived.append(
                    lax.ppermute(sources[which], "seq", swap_pairs(seq_count, across))
                )
            *sources, = lax.optimization_barrier((*sources, *arrived))
            sources, arrived = sources[:3], sources[3:]
            if step < planes - 1:
                proj_others.append(arrived[0])
                proj_blocks.append(arrived[1])
            if step < len(hops):
                gathered[which][across] = arrived[-1]
            if step == 0:
                targets = [target.T] + [around(sources[2], hop) for hop in range(1, planes)]
    depth_cut = depth // 2 if planes > 1 else depth
    last_other = [other_half(proj_blocks[-1][:depth_cut])]
    if planes > 1:
        last_other.append(around(proj_others[-1][depth_cut:]))
    for blocks in gathered:
        for across in range(0, seq_count, 2):
            blocks[across + 1] = other_core(blocks[across])
    key_blocks, value_blocks = gathered
    attended = attention(
        queries[0], key_blocks, value_blocks, HEADS, []
    )
    both_attended = jnp.concatenate([attended, other_core(attended)], axis=0)
    projected = 0.0
    for step in range(planes):
        own_at = source_plane[step] * HALVES + half
        other_at = source_plane[step] * HALVES + (1 - half)
        pieces = [(own_at * depth, proj_blocks[step])]
        if step < planes - 1:
            pieces.append((other_at * depth, proj_others[step]))
        else:
            pieces += [
                (other_at * depth + cut, block)
                for cut, block in zip((0, depth_cut), last_other)
            ]
        for at, block in pieces:
            columns = lax.dynamic_slice_in_dim(both_attended, at, block.shape[0], axis=1)
            projected = projected + jnp.dot(columns, block, preferred_element_type=jnp.float32)
    mine, theirs = projected[:row_count], other_core(projected[row_count:])
    projected = jnp.concatenate(
        [jnp.where(core == 0, mine, theirs), jnp.where(core == 0, theirs, mine)], axis=1
    )

    residual = hidden[0].astype(jnp.float32) + projected
    row_mean = jnp.mean(residual, axis=1, keepdims=True)
    centered = residual - row_mean
    row_var = jnp.mean(centered * centered, axis=1, keepdims=True)
    normed = (centered * lax.rsqrt(row_var + NORM_EPS) * ln_gain).astype(jnp.bfloat16)

    block_rows = seq_count * slot_count
    pair_rows = 2 * slot_count
    slot_ids = jnp.arange(block_rows, dtype=jnp.int32)
    served = jnp.bitwise_xor(slot_ids // slot_count, seq_at) * planes + plane
    served_target = served * slot_count + slot_ids % slot_count

    def exchange(rows):
        parts = [rows[i * slot_count : (i + 1) * slot_count] for i in range(seq_count)]
        for i in range(1, seq_count):
            parts[i] = lax.ppermute(parts[i], "seq", swap_pairs(seq_count, i))
        return tuple(parts)

    made = {}

    def get(name):
        if name not in made:
            made[name] = MAKE[name[0]](int(name[1:]), [get(other) for other in TIES.get(name, []) if int(other[1:]) < planes])
        return made[name]

    def tied(value, others):
        return after(value, [other[0] if isinstance(other, tuple) else other for other in others])

    def token_block(step, ties):
        return around(tied(get(f"Z{step - 1}"), ties)) if step else normed

    def matches(step):
        target = targets[step].T
        return [target[:, k : k + 1] == served_target[None, :] for k in range(2)]

    def slot_block(step, ties):
        match = matches(step)
        return jnp.einsum(
            "ts,td->sd",
            (match[0] | match[1]).astype(jnp.bfloat16),
            tied(get(f"Z{step}"), ties),
            preferred_element_type=jnp.float32,
        ).astype(jnp.bfloat16)

    def expert_rows(step, ties):
        return jnp.concatenate(exchange(tied(get(f"S{step}"), ties)), axis=0)

    def other_rows(step, ties):
        return other_half(tied(get(f"W{step}"), ties))

    def expert_out(step, ties):
        own, other = get(f"W{step}"), get(f"D{step}")
        ties = [tie[0] if isinstance(tie, tuple) else tie for tie in ties]
        return tuple(expert_half(own, other, w_in[0], w_out[0], ties))

    def other_out(step, ties):
        return other_half(tied(get(f"E{step}")[1], ties))

    def both_halves(step, ties):
        own = tied(get(f"E{step}")[0], ties)
        both = own.astype(jnp.float32) + get(f"R{step}").astype(jnp.float32)
        return both.astype(jnp.bfloat16)

    def returned_rows(step, ties):
        return exchange(tied(get(f"H{step}"), ties))

    def gated_part(step, ties):
        parts = get(f"X{step}")
        if ties:
            ties = [tie[0] if isinstance(tie, tuple) else tie for tie in ties]
            parts = lax.optimization_barrier((*parts, *ties))[: len(parts)]
        returned = jnp.concatenate(parts, axis=0)
        match = matches(step)
        logits = jnp.dot(get(f"Z{step}"), w_router, preferred_element_type=jnp.float32)
        named = (targets[step].T // slot_count)[:, :, None] == expert_ids[None, None, :]
        picked = jnp.sum(jnp.where(named, logits[:, None, :], 0.0), axis=2)
        gate_first = 1.0 / (1.0 + jnp.exp(picked[:, 1:2] - picked[:, 0:1]))
        gate_second = 1.0 / (1.0 + jnp.exp(picked[:, 0:1] - picked[:, 1:2]))
        gate_map = jnp.where(match[0], gate_first, 0.0) + jnp.where(match[1], gate_second, 0.0)
        gate_high = gate_map.astype(jnp.bfloat16)
        gate_low = (gate_map - gate_high.astype(jnp.float32)).astype(jnp.bfloat16)
        return jnp.dot(gate_high, returned, preferred_element_type=jnp.float32) + jnp.dot(
            gate_low, returned, preferred_element_type=jnp.float32
        )

    def passed_sum(step, ties):
        part = get(f"G{step}")
        if step > 1:
            part = part + around(get(f"P{step - 1}")).astype(jnp.float32)
        return tied(part.astype(jnp.bfloat16), ties)

    MAKE = {
        "Z": token_block,
        "S": slot_block,
        "W": expert_rows,
        "D": other_rows,
        "E": expert_out,
        "R": other_out,
        "H": both_halves,
        "X": returned_rows,
        "G": gated_part,
        "P": passed_sum,
    }
    layer_out = residual + get("G0")
    if planes > 1:
        last = get(f"P{planes - 1}")
        with jax.named_scope("home"):
            layer_out = layer_out + around(last).astype(jnp.float32)
    return layer_out.astype(jnp.bfloat16)[None]


def solution(mesh):
    seq_count, expert_dev = mesh.shape["seq"], mesh.shape["expert"]
    in_specs = (
        P("expert", "seq", None),
        P("expert", "seq", None),
        P("expert", "seq", None),
        P("expert", "seq", None),
        P("expert", None),
        P(),
        P(),
        P("expert", "seq", None),
        P(("seq", "expert"), None, None),
        P(("seq", "expert"), None, None),
    )
    out_specs = P("expert", "seq", None)

    def device_part(*arrays):
        return on_device(seq_count, expert_dev, *arrays)

    return jax.shard_map(
        device_part, mesh=mesh, in_specs=in_specs, out_specs=out_specs, check_vma=False
    )
```

```python
import functools

import jax
import jax.numpy as jnp
from jax import lax
from jax.experimental import pallas as pl
from jax.experimental.pallas import tpu as pltpu
from jax.sharding import PartitionSpec as P

HEADS = 16
HALVES = 2
TIES = {"E1": ["D0", "W2"], "E2": ["W3"], "H1": ["E2"], "H2": ["E3", "P1"], "H3": ["E0"], "E0": ["E3", "H2"], "X3": ["E0", "P2"], "S1": ["W0"], "Z2": ["W0"], "Z3": ["D0"], "G1": ["E3"]}
ECOST = 4000000000
ACOST = 1000


NORM_EPS = 1e-05


def line_ring(count):
    return [0] + list(range(1, count, 2)) + [i for i in range(count - 1, 0, -1) if i % 2 == 0]


def swap_pairs(count, offset):
    return [(i, i ^ offset) for i in range(count)]


def after(block, earlier):
    return lax.optimization_barrier((block, *earlier))[0] if earlier else block


def attention_kernel(block_count, head_dim, *refs):
    query_ref, key_refs = refs[0], refs[1 : 1 + block_count]
    value_refs, out_ref = refs[1 + block_count : 1 + 2 * block_count], refs[-1]
    source_count = key_refs[0].shape[0]
    heads = [
        slice(at * head_dim, (at + 1) * head_dim) for at in range(query_ref.shape[1] // head_dim)
    ]
    ones = jnp.ones((source_count, head_dim), jnp.bfloat16)
    scores = [
        [
            lax.dot_general(
                query_ref[:, head],
                key_ref[:, head],
                (((1,), (1,)), ((), ())),
                preferred_element_type=jnp.float32,
            )
            for key_ref in key_refs
        ]
        for head in heads
    ]
    tops = [
        jnp.max(functools.reduce(jnp.maximum, blocks), axis=1, keepdims=True) for blocks in scores
    ]
    weights = [
        [jnp.exp((block - top) * head_dim ** (-0.5)).astype(jnp.bfloat16) for block in blocks]
        for blocks, top in zip(scores, tops)
    ]
    for head, blocks in zip(heads, weights):
        sums = sum(
            jnp.dot(
                block,
                jnp.concatenate([value_ref[:, head], ones], axis=1),
                preferred_element_type=jnp.float32,
            )
            for block, value_ref in zip(blocks, value_refs)
        )
        out_ref[:, head] = (sums[:, :head_dim] / sums[:, head_dim:]).astype(out_ref.dtype)


VMEM_BYTES = 56 * 1024 * 1024
EXPERT_BYTES = 48 * 1024 * 1024


def attention(query_rows, key_blocks, value_blocks, head_count, earlier):
    row_count, model_width = query_rows.shape
    head_dim = model_width // head_count
    width = model_width // 4
    operands = [query_rows, *key_blocks, *value_blocks]
    return pl.pallas_call(
        functools.partial(attention_kernel, len(key_blocks), head_dim),
        grid=(model_width // width,),
        in_specs=[pl.BlockSpec((block.shape[0], width), lambda i: (0, i)) for block in operands]
        + [pl.BlockSpec(memory_space=pl.ANY) for _ in earlier],
        out_specs=pl.BlockSpec((row_count, width), lambda i: (0, i)),
        out_shape=jax.ShapeDtypeStruct((row_count, model_width), jnp.bfloat16),
        compiler_params=pltpu.CompilerParams(vmem_limit_bytes=VMEM_BYTES),
        cost_estimate=pl.CostEstimate(flops=ACOST, bytes_accessed=1000, transcendentals=0),
    )(*operands, *earlier)


def expert_kernel(own_ref, other_ref, first_ref, second_ref, *refs):
    own_out, other_out, rows, inner, outs, first, second, weight_sems, row_sems, out_sems = refs[-10:]
    count = own_ref.shape[0]
    tile = first.shape[1] // 2

    def columns(at):
        return pl.ds(at * tile, tile)

    weight_copies = [
        pltpu.make_async_copy(
            source.at[:, columns(at)], held.at[:, columns(at)], weight_sems.at[2 * which + at]
        )
        for which, (source, held) in enumerate(((first_ref, first), (second_ref, second)))
        for at in range(2)
    ]
    row_copies = [
        pltpu.make_async_copy(own_ref, rows.at[:count], row_sems.at[0]),
        pltpu.make_async_copy(other_ref, rows.at[count:], row_sems.at[1]),
    ]
    out_copies = [
        pltpu.make_async_copy(
            outs.at[which * count : (which + 1) * count, columns(at)],
            target.at[:, columns(at)],
            out_sems.at[2 * at + which],
        )
        for at in range(2)
        for which, target in enumerate((own_out, other_out))
    ]
    for copy in row_copies + weight_copies[:2]:
        copy.start()
    for copy in row_copies:
        copy.wait()
    for at in range(2):
        weight_copies[2 + at].start()
        weight_copies[at].wait()
        act = jnp.dot(rows[...], first[:, columns(at)], preferred_element_type=jnp.float32)
        inner[:, columns(at)] = jnp.maximum(act, 0.0).astype(inner.dtype)
    for at in range(2):
        weight_copies[2 + at].wait()
        outs[:, columns(at)] = jnp.dot(
            inner[...], second[:, columns(at)], preferred_element_type=jnp.float32
        ).astype(outs.dtype)
        for copy in out_copies[2 * at : 2 * at + 2]:
            copy.start()
    for copy in out_copies:
        copy.wait()


def expert_half(own_rows, other_rows, first, second, earlier):
    count, model_width = own_rows.shape
    hidden_width = first.shape[1]
    out_type = jax.ShapeDtypeStruct((count, model_width), jnp.bfloat16)
    anywhere = pl.BlockSpec(memory_space=pl.ANY)
    return pl.pallas_call(
        expert_kernel,
        in_specs=[anywhere] * (4 + len(earlier)),
        out_specs=[anywhere, anywhere],
        out_shape=[out_type, out_type],
        scratch_shapes=[
            pltpu.VMEM((2 * count, model_width), jnp.bfloat16),
            pltpu.VMEM((2 * count, hidden_width), jnp.bfloat16),
            pltpu.VMEM((2 * count, model_width), jnp.bfloat16),
            pltpu.VMEM(first.shape, jnp.bfloat16),
            pltpu.VMEM(second.shape, jnp.bfloat16),
            pltpu.SemaphoreType.DMA((4,)),
            pltpu.SemaphoreType.DMA((2,)),
            pltpu.SemaphoreType.DMA((4,)),
        ],
        compiler_params=pltpu.CompilerParams(vmem_limit_bytes=EXPERT_BYTES),
        cost_estimate=pl.CostEstimate(flops=ECOST, bytes_accessed=1000, transcendentals=0),
    )(own_rows, other_rows, first, second, *earlier)


def on_device(
    seq_count, expert_dev, queries, keys, values, hidden, out_proj, ln_gain, w_router, routes, w_in, w_out
):
    row_count, model_width = queries.shape[1:]
    expert_count = w_router.shape[1]
    slot_count = 4 * row_count // expert_count
    planes = expert_dev // HALVES
    seq_at = lax.axis_index("seq")
    expert_at = lax.axis_index("expert")
    plane, half = expert_at // HALVES, expert_at % HALVES
    core = seq_at % 2

    ring = line_ring(planes)
    ring_pairs = [
        [
            (ring[i] * HALVES + j, ring[(i + hop) % planes] * HALVES + j)
            for i in range(planes)
            for j in range(HALVES)
        ]
        for hop in range(planes)
    ]
    place_of = {ring[i]: i for i in range(planes)}
    source_plane = [
        sum(
            jnp.where(plane == i, ring[(place_of[i] - step) % planes], 0) for i in range(planes)
        )
        for step in range(planes)
    ]
    half_pairs = swap_pairs(expert_dev, 1)
    core_pairs = swap_pairs(seq_count, 1)

    def around(block, hop=1):
        with jax.named_scope("ring"):
            return lax.ppermute(block, "expert", ring_pairs[hop])

    def other_half(block):
        with jax.named_scope("half"):
            return lax.ppermute(block, "expert", half_pairs)

    def other_core(block):
        with jax.named_scope("core"):
            return lax.ppermute(block, "seq", core_pairs)

    chosen = routes[0].reshape(-1)
    expert_ids = jnp.arange(expert_count, dtype=jnp.int32)
    one_hot = (chosen[:, None] == expert_ids[None, :]).astype(jnp.int32)
    slot_index = jnp.sum(jnp.cumsum(one_hot, axis=0) * one_hot, axis=1) - 1
    target = (chosen * slot_count + slot_index).reshape(row_count, 2)

    depth = out_proj.shape[0]
    half_width = model_width // 2
    proj_part = lax.dynamic_slice_in_dim(out_proj, core * half_width, half_width, axis=1)
    proj_blocks, proj_others = [proj_part], []
    sources = [keys[0], values[0], target.T]
    gathered = [[source] + [None] * (seq_count - 1) for source in sources[:2]]
    hops = [(which, across) for which in range(2) for across in range(2, seq_count, 2)]
    for step in range(max(planes - 1, len(hops))):
        with jax.named_scope(f"gather_{step}"):
            arrived = []
            if step < planes - 1:
                arrived = [other_half(proj_blocks[step]), around(proj_blocks[step])]
            if step < len(hops):
                which, across = hops[step]
                arrived.append(
                    lax.ppermute(sources[which], "seq", swap_pairs(seq_count, across))
                )
            *sources, = lax.optimization_barrier((*sources, *arrived))
            sources, arrived = sources[:3], sources[3:]
            if step < planes - 1:
                proj_others.append(arrived[0])
                proj_blocks.append(arrived[1])
            if step < len(hops):
                gathered[which][across] = arrived[-1]
            if step == 0:
                targets = [target.T] + [around(sources[2], hop) for hop in range(1, planes)]
    depth_cut = depth // 2 if planes > 1 else depth
    last_other = [other_half(proj_blocks[-1][:depth_cut])]
    if planes > 1:
        last_other.append(around(proj_others[-1][depth_cut:]))
    for blocks in gathered:
        for across in range(0, seq_count, 2):
            blocks[across + 1] = other_core(blocks[across])
    key_blocks, value_blocks = gathered
    attended = attention(
        queries[0], key_blocks, value_blocks, HEADS, []
    )
    both_attended = jnp.concatenate([attended, other_core(attended)], axis=0)
    projected = 0.0
    for step in range(planes):
        own_at = source_plane[step] * HALVES + half
        other_at = source_plane[step] * HALVES + (1 - half)
        pieces = [(own_at * depth, proj_blocks[step])]
        if step < planes - 1:
            pieces.append((other_at * depth, proj_others[step]))
        else:
            pieces += [
                (other_at * depth + cut, block)
                for cut, block in zip((0, depth_cut), last_other)
            ]
        for at, block in pieces:
            columns = lax.dynamic_slice_in_dim(both_attended, at, block.shape[0], axis=1)
            projected = projected + jnp.dot(columns, block, preferred_element_type=jnp.float32)
    mine, theirs = projected[:row_count], other_core(projected[row_count:])
    projected = jnp.concatenate(
        [jnp.where(core == 0, mine, theirs), jnp.where(core == 0, theirs, mine)], axis=1
    )

    residual = hidden[0].astype(jnp.float32) + projected
    row_mean = jnp.mean(residual, axis=1, keepdims=True)
    centered = residual - row_mean
    row_var = jnp.mean(centered * centered, axis=1, keepdims=True)
    normed = (centered * lax.rsqrt(row_var + NORM_EPS) * ln_gain).astype(jnp.bfloat16)

    block_rows = seq_count * slot_count
    pair_rows = 2 * slot_count
    slot_ids = jnp.arange(block_rows, dtype=jnp.int32)
    served = jnp.bitwise_xor(slot_ids // slot_count, seq_at) * planes + plane
    served_target = served * slot_count + slot_ids % slot_count

    def exchange(rows):
        parts = [rows[i * slot_count : (i + 1) * slot_count] for i in range(seq_count)]
        for i in range(1, seq_count):
            parts[i] = lax.ppermute(parts[i], "seq", swap_pairs(seq_count, i))
        return tuple(parts)

    made = {}

    def get(name):
        if name not in made:
            made[name] = MAKE[name[0]](int(name[1:]), [get(other) for other in TIES.get(name, []) if int(other[1:]) < planes])
        return made[name]

    def tied(value, others):
        return after(value, [other[0] if isinstance(other, tuple) else other for other in others])

    def token_block(step, ties):
        return around(tied(get(f"Z{step - 1}"), ties)) if step else normed

    def matches(step):
        target = targets[step].T
        return [target[:, k : k + 1] == served_target[None, :] for k in range(2)]

    def slot_block(step, ties):
        match = matches(step)
        return jnp.einsum(
            "ts,td->sd",
            (match[0] | match[1]).astype(jnp.bfloat16),
            tied(get(f"Z{step}"), ties),
            preferred_element_type=jnp.float32,
        ).astype(jnp.bfloat16)

    def expert_rows(step, ties):
        return jnp.concatenate(exchange(tied(get(f"S{step}"), ties)), axis=0)

    def other_rows(step, ties):
        return other_half(tied(get(f"W{step}"), ties))

    def expert_out(step, ties):
        own, other = get(f"W{step}"), get(f"D{step}")
        ties = [tie[0] if isinstance(tie, tuple) else tie for tie in ties]
        return tuple(expert_half(own, other, w_in[0], w_out[0], ties))

    def other_out(step, ties):
        return other_half(tied(get(f"E{step}")[1], ties))

    def both_halves(step, ties):
        own = tied(get(f"E{step}")[0], ties)
        both = own.astype(jnp.float32) + get(f"R{step}").astype(jnp.float32)
        return both.astype(jnp.bfloat16)

    def returned_rows(step, ties):
        return exchange(tied(get(f"H{step}"), ties))

    def gated_part(step, ties):
        parts = get(f"X{step}")
        if ties:
            ties = [tie[0] if isinstance(tie, tuple) else tie for tie in ties]
            parts = lax.optimization_barrier((*parts, *ties))[: len(parts)]
        returned = jnp.concatenate(parts, axis=0)
        match = matches(step)
        logits = jnp.dot(get(f"Z{step}"), w_router, preferred_element_type=jnp.float32)
        named = (targets[step].T // slot_count)[:, :, None] == expert_ids[None, None, :]
        picked = jnp.sum(jnp.where(named, logits[:, None, :], 0.0), axis=2)
        gate_first = 1.0 / (1.0 + jnp.exp(picked[:, 1:2] - picked[:, 0:1]))
        gate_second = 1.0 / (1.0 + jnp.exp(picked[:, 0:1] - picked[:, 1:2]))
        gate_map = jnp.where(match[0], gate_first, 0.0) + jnp.where(match[1], gate_second, 0.0)
        gate_high = gate_map.astype(jnp.bfloat16)
        gate_low = (gate_map - gate_high.astype(jnp.float32)).astype(jnp.bfloat16)
        return jnp.dot(gate_high, returned, preferred_element_type=jnp.float32) + jnp.dot(
            gate_low, returned, preferred_element_type=jnp.float32
        )

    def passed_sum(step, ties):
        part = get(f"G{step}")
        if step > 1:
            part = part + around(get(f"P{step - 1}")).astype(jnp.float32)
        return tied(part.astype(jnp.bfloat16), ties)

    MAKE = {
        "Z": token_block,
        "S": slot_block,
        "W": expert_rows,
        "D": other_rows,
        "E": expert_out,
        "R": other_out,
        "H": both_halves,
        "X": returned_rows,
        "G": gated_part,
        "P": passed_sum,
    }
    layer_out = residual + get("G0")
    if planes > 1:
        last = get(f"P{planes - 1}")
        with jax.named_scope("home"):
            layer_out = layer_out + around(last).astype(jnp.float32)
    return layer_out.astype(jnp.bfloat16)[None]


def solution(mesh):
    seq_count, expert_dev = mesh.shape["seq"], mesh.shape["expert"]
    in_specs = (
        P("expert", "seq", None),
        P("expert", "seq", None),
        P("expert", "seq", None),
        P("expert", "seq", None),
        P("expert", None),
        P(),
        P(),
        P("expert", "seq", None),
        P(("seq", "expert"), None, None),
        P(("seq", "expert"), None, None),
    )
    out_specs = P("expert", "seq", None)

    def device_part(*arrays):
        return on_device(seq_count, expert_dev, *arrays)

    return jax.shard_map(
        device_part, mesh=mesh, in_specs=in_specs, out_specs=out_specs, check_vma=False
    )
```

```python
import functools

import jax
import jax.numpy as jnp
from jax import lax
from jax.experimental import pallas as pl
from jax.experimental.pallas import tpu as pltpu
from jax.sharding import PartitionSpec as P

HEADS = 16
HALVES = 2
TIES = {"E1": ["D0", "W2"], "E2": ["W3"], "H1": ["E2"], "H2": ["E3", "P1"], "H3": ["E0"], "E0": ["E3", "H2"], "X3": ["E0", "P2"], "S1": ["W0"], "Z2": ["W0"], "G1": ["E3"]}
ECOST = 4000000000
ACOST = 1000


NORM_EPS = 1e-05


def line_ring(count):
    return [0] + list(range(1, count, 2)) + [i for i in range(count - 1, 0, -1) if i % 2 == 0]


def swap_pairs(count, offset):
    return [(i, i ^ offset) for i in range(count)]


def after(block, earlier):
    return lax.optimization_barrier((block, *earlier))[0] if earlier else block


def attention_kernel(block_count, head_dim, *refs):
    query_ref, key_refs = refs[0], refs[1 : 1 + block_count]
    value_refs, out_ref = refs[1 + block_count : 1 + 2 * block_count], refs[-1]
    source_count = key_refs[0].shape[0]
    heads = [
        slice(at * head_dim, (at + 1) * head_dim) for at in range(query_ref.shape[1] // head_dim)
    ]
    ones = jnp.ones((source_count, head_dim), jnp.bfloat16)
    scores = [
        [
            lax.dot_general(
                query_ref[:, head],
                key_ref[:, head],
                (((1,), (1,)), ((), ())),
                preferred_element_type=jnp.float32,
            )
            for key_ref in key_refs
        ]
        for head in heads
    ]
    tops = [
        jnp.max(functools.reduce(jnp.maximum, blocks), axis=1, keepdims=True) for blocks in scores
    ]
    weights = [
        [jnp.exp((block - top) * head_dim ** (-0.5)).astype(jnp.bfloat16) for block in blocks]
        for blocks, top in zip(scores, tops)
    ]
    for head, blocks in zip(heads, weights):
        sums = sum(
            jnp.dot(
                block,
                jnp.concatenate([value_ref[:, head], ones], axis=1),
                preferred_element_type=jnp.float32,
            )
            for block, value_ref in zip(blocks, value_refs)
        )
        out_ref[:, head] = (sums[:, :head_dim] / sums[:, head_dim:]).astype(out_ref.dtype)


VMEM_BYTES = 56 * 1024 * 1024
EXPERT_BYTES = 48 * 1024 * 1024


def attention(query_rows, key_blocks, value_blocks, head_count, earlier):
    row_count, model_width = query_rows.shape
    head_dim = model_width // head_count
    width = model_width // 4
    operands = [query_rows, *key_blocks, *value_blocks]
    return pl.pallas_call(
        functools.partial(attention_kernel, len(key_blocks), head_dim),
        grid=(model_width // width,),
        in_specs=[pl.BlockSpec((block.shape[0], width), lambda i: (0, i)) for block in operands]
        + [pl.BlockSpec(memory_space=pl.ANY) for _ in earlier],
        out_specs=pl.BlockSpec((row_count, width), lambda i: (0, i)),
        out_shape=jax.ShapeDtypeStruct((row_count, model_width), jnp.bfloat16),
        compiler_params=pltpu.CompilerParams(vmem_limit_bytes=VMEM_BYTES),
        cost_estimate=pl.CostEstimate(flops=ACOST, bytes_accessed=1000, transcendentals=0),
    )(*operands, *earlier)


def expert_kernel(own_ref, other_ref, first_ref, second_ref, *refs):
    own_out, other_out, rows, inner, outs, first, second, weight_sems, row_sems, out_sems = refs[-10:]
    count = own_ref.shape[0]
    tile = first.shape[1] // 2

    def columns(at):
        return pl.ds(at * tile, tile)

    weight_copies = [
        pltpu.make_async_copy(
            source.at[:, columns(at)], held.at[:, columns(at)], weight_sems.at[2 * which + at]
        )
        for which, (source, held) in enumerate(((first_ref, first), (second_ref, second)))
        for at in range(2)
    ]
    row_copies = [
        pltpu.make_async_copy(own_ref, rows.at[:count], row_sems.at[0]),
        pltpu.make_async_copy(other_ref, rows.at[count:], row_sems.at[1]),
    ]
    out_copies = [
        pltpu.make_async_copy(
            outs.at[which * count : (which + 1) * count, columns(at)],
            target.at[:, columns(at)],
            out_sems.at[2 * at + which],
        )
        for at in range(2)
        for which, target in enumerate((own_out, other_out))
    ]
    for copy in row_copies + weight_copies[:2]:
        copy.start()
    for copy in row_copies:
        copy.wait()
    for at in range(2):
        weight_copies[2 + at].start()
        weight_copies[at].wait()
        act = jnp.dot(rows[...], first[:, columns(at)], preferred_element_type=jnp.float32)
        inner[:, columns(at)] = jnp.maximum(act, 0.0).astype(inner.dtype)
    for at in range(2):
        weight_copies[2 + at].wait()
        outs[:, columns(at)] = jnp.dot(
            inner[...], second[:, columns(at)], preferred_element_type=jnp.float32
        ).astype(outs.dtype)
        for copy in out_copies[2 * at : 2 * at + 2]:
            copy.start()
    for copy in out_copies:
        copy.wait()


def expert_half(own_rows, other_rows, first, second, earlier):
    count, model_width = own_rows.shape
    hidden_width = first.shape[1]
    out_type = jax.ShapeDtypeStruct((count, model_width), jnp.bfloat16)
    anywhere = pl.BlockSpec(memory_space=pl.ANY)
    return pl.pallas_call(
        expert_kernel,
        in_specs=[anywhere] * (4 + len(earlier)),
        out_specs=[anywhere, anywhere],
        out_shape=[out_type, out_type],
        scratch_shapes=[
            pltpu.VMEM((2 * count, model_width), jnp.bfloat16),
            pltpu.VMEM((2 * count, hidden_width), jnp.bfloat16),
            pltpu.VMEM((2 * count, model_width), jnp.bfloat16),
            pltpu.VMEM(first.shape, jnp.bfloat16),
            pltpu.VMEM(second.shape, jnp.bfloat16),
            pltpu.SemaphoreType.DMA((4,)),
            pltpu.SemaphoreType.DMA((2,)),
            pltpu.SemaphoreType.DMA((4,)),
        ],
        compiler_params=pltpu.CompilerParams(vmem_limit_bytes=EXPERT_BYTES),
        cost_estimate=pl.CostEstimate(flops=ECOST, bytes_accessed=1000, transcendentals=0),
    )(own_rows, other_rows, first, second, *earlier)


def on_device(
    seq_count, expert_dev, queries, keys, values, hidden, out_proj, ln_gain, w_router, routes, w_in, w_out
):
    row_count, model_width = queries.shape[1:]
    expert_count = w_router.shape[1]
    slot_count = 4 * row_count // expert_count
    planes = expert_dev // HALVES
    seq_at = lax.axis_index("seq")
    expert_at = lax.axis_index("expert")
    plane, half = expert_at // HALVES, expert_at % HALVES
    core = seq_at % 2

    ring = line_ring(planes)
    ring_pairs = [
        [
            (ring[i] * HALVES + j, ring[(i + hop) % planes] * HALVES + j)
            for i in range(planes)
            for j in range(HALVES)
        ]
        for hop in range(planes)
    ]
    place_of = {ring[i]: i for i in range(planes)}
    source_plane = [
        sum(
            jnp.where(plane == i, ring[(place_of[i] - step) % planes], 0) for i in range(planes)
        )
        for step in range(planes)
    ]
    half_pairs = swap_pairs(expert_dev, 1)
    core_pairs = swap_pairs(seq_count, 1)

    def around(block, hop=1):
        with jax.named_scope("ring"):
            return lax.ppermute(block, "expert", ring_pairs[hop])

    def other_half(block):
        with jax.named_scope("half"):
            return lax.ppermute(block, "expert", half_pairs)

    def other_core(block):
        with jax.named_scope("core"):
            return lax.ppermute(block, "seq", core_pairs)

    chosen = routes[0].reshape(-1)
    expert_ids = jnp.arange(expert_count, dtype=jnp.int32)
    one_hot = (chosen[:, None] == expert_ids[None, :]).astype(jnp.int32)
    slot_index = jnp.sum(jnp.cumsum(one_hot, axis=0) * one_hot, axis=1) - 1
    target = (chosen * slot_count + slot_index).reshape(row_count, 2)

    depth = out_proj.shape[0]
    half_width = model_width // 2
    proj_part = lax.dynamic_slice_in_dim(out_proj, core * half_width, half_width, axis=1)
    proj_blocks, proj_others = [proj_part], []
    sources = [keys[0], values[0], target.T]
    gathered = [[source] + [None] * (seq_count - 1) for source in sources[:2]]
    hops = [(which, across) for which in range(2) for across in range(2, seq_count, 2)]
    for step in range(max(planes - 1, len(hops))):
        with jax.named_scope(f"gather_{step}"):
            arrived = []
            if step < planes - 1:
                arrived = [other_half(proj_blocks[step]), around(proj_blocks[step])]
            if step < len(hops):
                which, across = hops[step]
                arrived.append(
                    lax.ppermute(sources[which], "seq", swap_pairs(seq_count, across))
                )
            *sources, = lax.optimization_barrier((*sources, *arrived))
            sources, arrived = sources[:3], sources[3:]
            if step < planes - 1:
                proj_others.append(arrived[0])
                proj_blocks.append(arrived[1])
            if step < len(hops):
                gathered[which][across] = arrived[-1]
            if step == 0:
                targets = [target.T] + [around(sources[2], hop) for hop in range(1, planes)]
    depth_cut = depth // 2 if planes > 1 else depth
    last_other = [other_half(proj_blocks[-1][:depth_cut])]
    if planes > 1:
        last_other.append(around(proj_others[-1][depth_cut:]))
    for blocks in gathered:
        for across in range(0, seq_count, 2):
            blocks[across + 1] = other_core(blocks[across])
    key_blocks, value_blocks = gathered
    attended = attention(
        queries[0], key_blocks, value_blocks, HEADS, []
    )
    both_attended = jnp.concatenate([attended, other_core(attended)], axis=0)
    projected = 0.0
    for step in range(planes):
        own_at = source_plane[step] * HALVES + half
        other_at = source_plane[step] * HALVES + (1 - half)
        pieces = [(own_at * depth, proj_blocks[step])]
        if step < planes - 1:
            pieces.append((other_at * depth, proj_others[step]))
        else:
            pieces += [
                (other_at * depth + cut, block)
                for cut, block in zip((0, depth_cut), last_other)
            ]
        for at, block in pieces:
            columns = lax.dynamic_slice_in_dim(both_attended, at, block.shape[0], axis=1)
            projected = projected + jnp.dot(columns, block, preferred_element_type=jnp.float32)
    mine, theirs = projected[:row_count], other_core(projected[row_count:])
    projected = jnp.concatenate(
        [jnp.where(core == 0, mine, theirs), jnp.where(core == 0, theirs, mine)], axis=1
    )

    residual = hidden[0].astype(jnp.float32) + projected
    row_mean = jnp.mean(residual, axis=1, keepdims=True)
    centered = residual - row_mean
    row_var = jnp.mean(centered * centered, axis=1, keepdims=True)
    normed = (centered * lax.rsqrt(row_var + NORM_EPS) * ln_gain).astype(jnp.bfloat16)

    block_rows = seq_count * slot_count
    pair_rows = 2 * slot_count
    slot_ids = jnp.arange(block_rows, dtype=jnp.int32)
    served = jnp.bitwise_xor(slot_ids // slot_count, seq_at) * planes + plane
    served_target = served * slot_count + slot_ids % slot_count

    def exchange(rows):
        parts = [rows[i * slot_count : (i + 1) * slot_count] for i in range(seq_count)]
        for i in range(1, seq_count):
            parts[i] = lax.ppermute(parts[i], "seq", swap_pairs(seq_count, i))
        return tuple(parts)

    made = {}

    def get(name):
        if name not in made:
            made[name] = MAKE[name[0]](int(name[1:]), [get(other) for other in TIES.get(name, []) if int(other[1:]) < planes])
        return made[name]

    def tied(value, others):
        return after(value, [other[0] if isinstance(other, tuple) else other for other in others])

    def token_block(step, ties):
        return around(tied(get(f"Z{step - 1}"), ties)) if step else normed

    def matches(step):
        target = targets[step].T
        return [target[:, k : k + 1] == served_target[None, :] for k in range(2)]

    def slot_block(step, ties):
        match = matches(step)
        return jnp.einsum(
            "ts,td->sd",
            (match[0] | match[1]).astype(jnp.bfloat16),
            tied(get(f"Z{step}"), ties),
            preferred_element_type=jnp.float32,
        ).astype(jnp.bfloat16)

    def expert_rows(step, ties):
        return jnp.concatenate(exchange(tied(get(f"S{step}"), ties)), axis=0)

    def other_rows(step, ties):
        return other_half(tied(get(f"W{step}"), ties))

    def expert_out(step, ties):
        own, other = get(f"W{step}"), get(f"D{step}")
        ties = [tie[0] if isinstance(tie, tuple) else tie for tie in ties]
        return tuple(expert_half(own, other, w_in[0], w_out[0], ties))

    def other_out(step, ties):
        return other_half(tied(get(f"E{step}")[1], ties))

    def both_halves(step, ties):
        own = tied(get(f"E{step}")[0], ties)
        both = own.astype(jnp.float32) + get(f"R{step}").astype(jnp.float32)
        return both.astype(jnp.bfloat16)

    def returned_rows(step, ties):
        return exchange(tied(get(f"H{step}"), ties))

    def gated_part(step, ties):
        parts = get(f"X{step}")
        if ties:
            ties = [tie[0] if isinstance(tie, tuple) else tie for tie in ties]
            parts = lax.optimization_barrier((*parts, *ties))[: len(parts)]
        returned = jnp.concatenate(parts, axis=0)
        match = matches(step)
        logits = jnp.dot(get(f"Z{step}"), w_router, preferred_element_type=jnp.float32)
        named = (targets[step].T // slot_count)[:, :, None] == expert_ids[None, None, :]
        picked = jnp.sum(jnp.where(named, logits[:, None, :], 0.0), axis=2)
        gate_first = 1.0 / (1.0 + jnp.exp(picked[:, 1:2] - picked[:, 0:1]))
        gate_second = 1.0 / (1.0 + jnp.exp(picked[:, 0:1] - picked[:, 1:2]))
        gate_map = jnp.where(match[0], gate_first, 0.0) + jnp.where(match[1], gate_second, 0.0)
        gate_high = gate_map.astype(jnp.bfloat16)
        gate_low = (gate_map - gate_high.astype(jnp.float32)).astype(jnp.bfloat16)
        return jnp.dot(gate_high, returned, preferred_element_type=jnp.float32) + jnp.dot(
            gate_low, returned, preferred_element_type=jnp.float32
        )

    def passed_sum(step, ties):
        part = get(f"G{step}")
        if step > 1:
            part = part + around(get(f"P{step - 1}")).astype(jnp.float32)
        return tied(part.astype(jnp.bfloat16), ties)

    MAKE = {
        "Z": token_block,
        "S": slot_block,
        "W": expert_rows,
        "D": other_rows,
        "E": expert_out,
        "R": other_out,
        "H": both_halves,
        "X": returned_rows,
        "G": gated_part,
        "P": passed_sum,
    }
    layer_out = residual + get("G0")
    if planes > 1:
        last = get(f"P{planes - 1}")
        with jax.named_scope("home"):
            layer_out = layer_out + around(last).astype(jnp.float32)
    return layer_out.astype(jnp.bfloat16)[None]


def solution(mesh):
    seq_count, expert_dev = mesh.shape["seq"], mesh.shape["expert"]
    in_specs = (
        P("expert", "seq", None),
        P("expert", "seq", None),
        P("expert", "seq", None),
        P("expert", "seq", None),
        P("expert", None),
        P(),
        P(),
        P("expert", "seq", None),
        P(("seq", "expert"), None, None),
        P(("seq", "expert"), None, None),
    )
    out_specs = P("expert", "seq", None)

    def device_part(*arrays):
        return on_device(seq_count, expert_dev, *arrays)

    return jax.shard_map(
        device_part, mesh=mesh, in_specs=in_specs, out_specs=out_specs, check_vma=False
    )
```
